512 devices in a mesh: pipe: 64 (over z_hi, x, y), tensor: 8 (over z_lo, core).
Axes of the slice: x: 4, y: 8, z: 8 (z_hi: 2, z_lo: 4; z = z_hi * 4 + z_lo), core: 2. Of those that a mesh axis runs over, the one named last changes fastest.
Arguments:
- inputs_a: bfloat16 [64, 224, 7168], P('pipe', None, 'tensor'), may hold values from -110 to 110
- inputs_b: bfloat16 [64, 224, 7168], P('pipe', None, 'tensor'), may hold values from -110 to 110
- sent_a: bfloat16 [64, 224, 7168], P('pipe', None, 'tensor'), may hold values from -6 to 6
- sent_b: bfloat16 [64, 224, 7168], P('pipe', None, 'tensor'), may hold values from -6 to 6
- gain_pair: float32 [64, 2, 7168], P('pipe', None, 'tensor'), may hold values from 0.5 to 2, as said below
- latent_gain_pair: float32 [64, 2, 256], P('pipe'), may hold values from 0.5 to 2, as said below
- compress_pair: bfloat16 [64, 2, 256, 7168], P('pipe', None, None, 'tensor'), as said below
- expand_pair: bfloat16 [64, 2, 256, 7168], P('pipe', None, None, 'tensor'), as said below
Outputs:
- input_grad_a: bfloat16 [64, 224, 7168], P('pipe', None, 'tensor')
- input_grad_b: bfloat16 [64, 224, 7168], P('pipe', None, 'tensor')
- grad_compress: bfloat16 [64, 256, 7168], P('pipe', None, 'tensor')
- grad_expand: bfloat16 [64, 256, 7168], P('pipe', None, 'tensor')
The draws below stay inside these ranges and needn't reach their ends.
Inputs may be any that keep to these rules, and one draw needn't show every extreme that they name: gain_pair[r, 1] equals gain_pair[63 - r, 0] for every rank r. latent_gain_pair[r, 1] equals latent_gain_pair[63 - r, 0] for every rank r. compress_pair[r, 1] equals compress_pair[63 - r, 0] for every rank r. expand_pair[r, 1] equals expand_pair[63 - r, 0] for every rank r.
All inputs are finite; a program needn't handle non-finite values.
Results may differ from the reference program's by a relative error of at most 0.0061.
Values may be sent and summed in bfloat16 or wider, within the bound.
No kernel may reach another device: no remote copies, remote signals or barrier semaphores. Data moves between devices by JAX's collectives and lax.ppermute only.
A program may use at most 64 MiB of HBM per device.

```python
import math
import jax
import jax.numpy as jnp
from jax import lax

D = 7168
R = 256
TOK = 224
SECTIONS = 64


def feature_scales(key, top_scale):
    rising = jnp.exp(jnp.linspace(0.0, math.log(top_scale), D))
    jitter = jnp.exp(jax.random.uniform(key, (D,), minval=math.log(0.5), maxval=math.log(2.0)))
    return rising * jitter


def scale_rows(key, raw_values, top_scale):
    row_scales = jnp.exp(jax.random.uniform(jax.random.fold_in(key, 1), raw_values.shape[:-1] + (1,), minval=math.log(0.3), maxval=math.log(3.0)))
    return (raw_values * row_scales * feature_scales(jax.random.fold_in(key, 2), top_scale)).astype(jnp.bfloat16)


def mirrored_normal(key, full_shape, spread):
    raw_values = jnp.clip(jax.random.normal(key, full_shape), -6.0, 6.0) * spread
    return jnp.stack([raw_values, jnp.flip(raw_values, 0)], axis=1)


def mirrored_gains(key, width):
    raw_values = jnp.exp(jax.random.uniform(key, (SECTIONS, width), minval=math.log(0.5), maxval=math.log(2.0)))
    return jnp.stack([raw_values, jnp.flip(raw_values, 0)], axis=1).astype(jnp.float32)


def draw_inputs_a(key, part):
    key = jax.random.fold_in(key, 11)
    full_shape = (SECTIONS, TOK, D)
    raw_values = jnp.clip(jax.random.normal(key, full_shape), -6.0, 6.0)
    top_scale = 3.0
    return scale_rows(jax.random.fold_in(key, 7), raw_values, top_scale)


def draw_inputs_b(key, part):
    key = jax.random.fold_in(key, 12)
    full_shape = (SECTIONS, TOK, D)
    raw_values = jnp.clip(jax.random.normal(key, full_shape), -6.0, 6.0)
    top_scale = 3.0
    return scale_rows(jax.random.fold_in(key, 7), raw_values, top_scale)


def draw_gain_pair(key, part):
    key = jax.random.fold_in(key, 13)
    return mirrored_gains(key, D)


def draw_latent_gain_pair(key, part):
    key = jax.random.fold_in(key, 17)
    return mirrored_gains(key, R)


def draw_compress_pair(key, part):
    key = jax.random.fold_in(key, 21)
    return mirrored_normal(key, (SECTIONS, R, D), D ** (-0.5)).astype(jnp.bfloat16)


def draw_expand_pair(key, part):
    key = jax.random.fold_in(key, 23)
    return mirrored_normal(key, (SECTIONS, R, D), R ** (-0.5)).astype(jnp.bfloat16)


def steps_of(stream_key, dims, split, least, top_value):
    def one(axis_at, blocks):
        steps = jax.random.uniform(jax.random.fold_in(jax.random.fold_in(stream_key, 6), axis_at), (blocks,), jnp.float32, least / len(split), top_value / len(split))
        return jnp.repeat(jnp.exp(steps), dims[axis_at] // blocks).reshape((-1,) + (1,) * (len(dims) - axis_at - 1))

    level = one(*split[0])
    for cut in split[1:]:
        level = level * one(*cut)
    return level


def scatter_about(rng, shape, scale, reach, split=(), held_as=jnp.bfloat16):
    gain = steps_of(rng, shape, split, -0.22, 0.18) if split else 1.0
    entries = jax.random.normal(rng, shape, jnp.float32) * scale * gain
    return jnp.minimum(jnp.maximum(entries, -reach), reach).astype(held_as)


def setup_inputs(seed: int = 0) -> dict:
    key_list = jax.random.split(jax.random.key(seed), 9)
    inputs_a = draw_inputs_a(jax.random.fold_in(key_list[8], 71), 0)
    inputs_b = draw_inputs_b(jax.random.fold_in(key_list[8], 71), 0)
    sent_a = scatter_about(key_list[2], (SECTIONS, TOK, D), 1.0, 6.0, ((0, 64), (2, 8)))
    sent_b = scatter_about(key_list[3], (SECTIONS, TOK, D), 1.0, 6.0, ((0, 64), (2, 8)))
    gain_pair = draw_gain_pair(jax.random.fold_in(key_list[8], 71), 0)
    latent_gain_pair = draw_latent_gain_pair(jax.random.fold_in(key_list[8], 71), 0)
    compress_pair = draw_compress_pair(jax.random.fold_in(key_list[8], 71), 0)
    expand_pair = draw_expand_pair(jax.random.fold_in(key_list[8], 71), 0)
    return dict(inputs_a=inputs_a, inputs_b=inputs_b, sent_a=sent_a, sent_b=sent_b, gain_pair=gain_pair, latent_gain_pair=latent_gain_pair, compress_pair=compress_pair, expand_pair=expand_pair)


EPSILON = 1e-06

def section_backward(inputs, cotangent, gain_row, latent_gain, w_compress, w_expand):
    values = inputs.astype(jnp.float32)
    rms_rows = jnp.sqrt(lax.optimization_barrier(jnp.mean(values * values, -1, keepdims=True)) + EPSILON)
    unit_rows = values / rms_rows
    normed = (unit_rows * gain_row).astype(jnp.bfloat16)
    latent = jnp.dot(normed, w_compress.T, preferred_element_type=jnp.float32)
    latent_rms = jnp.sqrt(lax.optimization_barrier(jnp.mean(latent * latent, -1, keepdims=True)) + EPSILON)
    latent_unit = latent / latent_rms
    latent_code = (latent_unit * latent_gain).astype(jnp.bfloat16)
    grad_code = jnp.dot(cotangent, w_expand.T, preferred_element_type=jnp.float32)
    grad_unit = grad_code * latent_gain
    latent_centre = lax.optimization_barrier(jnp.mean(grad_unit * latent_unit, -1, keepdims=True))
    grad_latent = ((grad_unit - latent_unit * latent_centre) / latent_rms).astype(jnp.bfloat16)
    grad_normed = jnp.dot(grad_latent, w_compress, preferred_element_type=jnp.float32)
    scaled = grad_normed * gain_row
    centre = lax.optimization_barrier(jnp.mean(scaled * unit_rows, -1, keepdims=True))
    input_grad = (cotangent.astype(jnp.float32) + (scaled - unit_rows * centre) / rms_rows).astype(jnp.bfloat16)
    compress_term = jnp.dot(grad_latent.T, normed, preferred_element_type=jnp.float32)
    expand_term = jnp.dot(latent_code.T, cotangent, preferred_element_type=jnp.float32)
    return (input_grad, compress_term, expand_term)

def reference(inputs_a, inputs_b, sent_a, sent_b, gain_pair, latent_gain_pair, compress_pair, expand_pair):
    cot_a = jnp.roll(sent_a, -1, axis=0)
    cot_b = jnp.roll(sent_b, 1, axis=0)
    section_items = (inputs_a, cot_a, gain_pair[:, 0], latent_gain_pair[:, 0], compress_pair[:, 0], expand_pair[:, 0], inputs_b, cot_b, gain_pair[:, 1], latent_gain_pair[:, 1], compress_pair[:, 1], expand_pair[:, 1])

    def one_rank(items):
        stream_one = section_backward(items[0], items[1], items[2], items[3], items[4], items[5])
        stream_two = section_backward(items[6], items[7], items[8], items[9], items[10], items[11])
        mirror_compress = lax.optimization_barrier(stream_two[1].astype(jnp.bfloat16))
        mirror_expand = lax.optimization_barrier(stream_two[2].astype(jnp.bfloat16))
        return (stream_one[0], stream_two[0], stream_one[1], stream_one[2], mirror_compress, mirror_expand)
    input_grad_a, input_grad_b, own_compress, own_expand, mirror_compress, mirror_expand = lax.map(one_rank, section_items)
    grad_compress = (own_compress + jnp.flip(mirror_compress, 0).astype(jnp.float32)).astype(jnp.bfloat16)
    grad_expand = (own_expand + jnp.flip(mirror_expand, 0).astype(jnp.float32)).astype(jnp.bfloat16)
    return (input_grad_a, input_grad_b, grad_compress, grad_expand)
```

```python
import jax
import jax.numpy as jnp
from jax import lax
from jax.experimental import pallas as pl
from jax.experimental.pallas import tpu as pltpu
from jax.sharding import PartitionSpec as P

EPSILON = 1e-06
TOKENS = 224
PADDED = 256
HALF = 128
PART = 32
WIDTH = 896
UNITS = 256
FEATURES = 7168
SUM_COLS = 4 * UNITS + 128
OWN_COLS = 3 * UNITS + 128
MIR_COLS = 2 * UNITS
ALL_COLS = OWN_COLS + MIR_COLS
F32 = jnp.float32
BF16 = jnp.bfloat16


def contract_last(left, right):
    return lax.dot_general(left, right, (((1,), (1,)), ((), ())), preferred_element_type=F32)


def contract_first(left, right):
    return lax.dot_general(left, right, (((0,), (0,)), ((), ())), preferred_element_type=F32)


def lanes(rows):
    return lax.broadcasted_iota(jnp.int32, (rows, 128), 1)


def split_pair(first, second):
    lane = lanes(first.shape[0])
    value = jnp.where(lane % 2 == 0, first, second)
    high = value.astype(BF16).astype(F32)
    packed = jnp.where(lane < 2, high, value - high)
    return jnp.where(lane < 4, packed, 0.0).astype(BF16)


def joined(block):
    block = block.astype(F32)
    return block[:, 0:1] + block[:, 2:3], block[:, 1:2] + block[:, 3:4]


def latent_kernel(xa_ref, xb_ref, gain_ref, wc_ref, xga_ref, xgb_ref, lat_ref):
    squares = []
    for s, (x_ref, xg_ref) in enumerate(((xa_ref, xga_ref), (xb_ref, xgb_ref))):
        x = x_ref[0].astype(F32)
        xg = (x * gain_ref[0, s : s + 1, :]).astype(BF16)
        xg_ref[...] = xg
        lat_ref[0:TOKENS, s * UNITS : (s + 1) * UNITS] = contract_last(xg, wc_ref[0, s])
        squares.append(jnp.sum(x * x, -1, keepdims=True))
    lane = lanes(TOKENS)
    block = jnp.where(lane == 0, squares[0], jnp.where(lane == 1, squares[1], 0.0))
    lat_ref[0:TOKENS, 2 * UNITS :] = block
    lat_ref[TOKENS:, :] = jnp.zeros((PADDED - TOKENS, 2 * UNITS + 128), F32)


def code_kernel(ca_ref, cb_ref, we_ref, lat_ref, keep_ref, send_ref, full):
    for s, c_ref in enumerate((ca_ref, cb_ref)):
        full[0:TOKENS, s * UNITS : (s + 1) * UNITS] = contract_last(c_ref[0], we_ref[0, s])
    full[TOKENS:, :] = jnp.zeros((PADDED - TOKENS, 2 * UNITS), F32)
    core = lax.rem(lax.axis_index("tensor"), 2)
    mine = pl.ds(pl.multiple_of(core * HALF, HALF), HALF)
    other = pl.ds(pl.multiple_of((1 - core) * HALF, HALF), HALF)
    keep_ref[:, 0 : 2 * UNITS] = lat_ref[mine, 0 : 2 * UNITS]
    keep_ref[:, 2 * UNITS : 4 * UNITS] = full[mine, :]
    keep_ref[:, 4 * UNITS :] = lat_ref[mine, 2 * UNITS :]
    send_ref[:, 0 : 2 * UNITS] = lat_ref[other, 0 : 2 * UNITS].astype(BF16)
    send_ref[:, 2 * UNITS : 4 * UNITS] = full[other, :].astype(BF16)
    block = lat_ref[other, 2 * UNITS :]
    send_ref[:, 4 * UNITS :] = split_pair(block[:, 0:1], block[:, 1:2])


def scatter_kernel(keep_ref, recv_ref, own_ref, one_ref, two_ref, three_ref, total):
    total[...] = keep_ref[...] + recv_ref[...].astype(F32)
    spot = lax.div(lax.axis_index("tensor"), 2)

    def rows(d):
        return pl.ds(pl.multiple_of((spot ^ d) * PART, PART), PART)

    own_ref[...] = total[rows(0), :]
    for d, ref in ((1, one_ref), (2, two_ref), (3, three_ref)):
        ref[:, 0 : 4 * UNITS] = total[rows(d), 0 : 4 * UNITS].astype(BF16)
        ref[:, 4 * UNITS :] = split_pair(*joined(total[rows(d), 4 * UNITS :]))


def latent_backward(latent_sum, grad_code, square, latent_gain):
    rms = jnp.sqrt(square / FEATURES + EPSILON)
    latent = latent_sum / rms
    latent_rms = jnp.sqrt(jnp.mean(latent * latent, -1, keepdims=True) + EPSILON)
    latent_unit = latent / latent_rms
    code = (latent_unit * latent_gain).astype(BF16)
    grad_unit = grad_code * latent_gain
    latent_centre = jnp.mean(grad_unit * latent_unit, -1, keepdims=True)
    grad_latent = (grad_unit - latent_unit * latent_centre) / latent_rms
    ratio = (grad_latent / rms).astype(BF16)
    centre = jnp.sum(ratio.astype(F32) * latent, -1, keepdims=True) / FEATURES / rms
    return ratio, code, centre


def latent_step_kernel(own_ref, one_ref, two_ref, three_ref, gain_ref, out_ref, mir_ref):
    total = own_ref[...]
    for ref in (one_ref, two_ref, three_ref):
        total = total + ref[...].astype(F32)
    square_a, square_b = joined(total[:, 4 * UNITS :])
    ratio_a, code_a, centre_a = latent_backward(
        total[:, 0:UNITS], total[:, 2 * UNITS : 3 * UNITS], square_a, gain_ref[0, 0:1, :]
    )
    ratio_b, code_b, centre_b = latent_backward(
        total[:, UNITS : 2 * UNITS], total[:, 3 * UNITS : 4 * UNITS], square_b, gain_ref[0, 1:2, :]
    )
    out_ref[:, 0:UNITS] = ratio_a
    out_ref[:, UNITS : 2 * UNITS] = code_a
    out_ref[:, 2 * UNITS : 3 * UNITS] = ratio_b
    out_ref[:, 3 * UNITS :] = split_pair(centre_a, centre_b)
    mir_ref[:, 0:UNITS] = ratio_b
    mir_ref[:, UNITS:] = code_b


def gather_kernel(own_ref, one_ref, two_ref, three_ref, out_ref):
    spot = lax.div(lax.axis_index("tensor"), 2)
    for d, ref in enumerate((own_ref, one_ref, two_ref, three_ref)):
        out_ref[pl.ds(pl.multiple_of((spot ^ d) * PART, PART), PART), :] = ref[...]


def finish_kernel(
    mine_ref, other_ref, ca_ref, cb_ref, xa_ref, xb_ref, xga_ref, xm_ref, cm_ref, gain_ref, wc_ref,
    ia_ref, ib_ref, gc_ref, ge_ref, full,
):
    core = lax.rem(lax.axis_index("tensor"), 2)
    full[pl.ds(pl.multiple_of(core * HALF, HALF), HALF), :] = mine_ref[...]
    full[pl.ds(pl.multiple_of((1 - core) * HALF, HALF), HALF), :] = other_ref[...]
    ratio_a = full[0:TOKENS, 0:UNITS]
    code_a = full[0:TOKENS, UNITS : 2 * UNITS]
    ratio_b = full[0:TOKENS, 2 * UNITS : 3 * UNITS]
    centres = joined(full[0:TOKENS, 3 * UNITS : OWN_COLS])
    ratio_m = full[0:TOKENS, OWN_COLS : OWN_COLS + UNITS]
    code_m = full[0:TOKENS, OWN_COLS + UNITS :]
    streams = ((ratio_a, ca_ref, xa_ref, ia_ref), (ratio_b, cb_ref, xb_ref, ib_ref))
    for s, (ratio, c_ref, x_ref, i_ref) in enumerate(streams):
        grad = jnp.dot(ratio, wc_ref[0, s], preferred_element_type=F32) * gain_ref[0, s : s + 1, :]
        i_ref[0] = (
            c_ref[0].astype(F32) + (grad - x_ref[0].astype(F32) * centres[s])
        ).astype(BF16)
    xg_m = (xm_ref[0].astype(F32) * gain_ref[0, 0:1, :]).astype(BF16)
    mirror = contract_first(ratio_m, xg_m).astype(BF16).astype(F32)
    gc_ref[0] = (contract_first(ratio_a, xga_ref[...]) + mirror).astype(BF16)
    mirror = contract_first(code_m, cm_ref[0]).astype(BF16).astype(F32)
    ge_ref[0] = (contract_first(code_a, ca_ref[0]) + mirror).astype(BF16)


def call(kernel, outs, scratch=(), flops=0, name=None):
    return pl.pallas_call(
        kernel,
        out_shape=[jax.ShapeDtypeStruct(shape, dtype) for shape, dtype in outs],
        scratch_shapes=[pltpu.VMEM(shape, dtype) for shape, dtype in scratch],
        compiler_params=pltpu.CompilerParams(vmem_limit_bytes=40 * 2**20),
        cost_estimate=pl.CostEstimate(flops=flops, bytes_accessed=4 * 2**20, transcendentals=0),
        name=name,
    )


def shards(xa, xb, sent_a, sent_b, gain, latent_gain, wc, we):
    pipe = range(lax.axis_size("pipe"))
    last = len(pipe) - 1
    tensor = range(lax.axis_size("tensor"))

    def swap(value, d):
        return lax.ppermute(value, "tensor", [(i, i ^ d) for i in tensor])

    ca = lax.ppermute(sent_a, "pipe", [((i + 1) % len(pipe), i) for i in pipe])
    cb = lax.ppermute(sent_b, "pipe", [(i, (i + 1) % len(pipe)) for i in pipe])
    xm = lax.ppermute(xb, "pipe", [(i, last - i) for i in pipe])
    cm = lax.ppermute(sent_b, "pipe", [(i, (last - 1 - i) % len(pipe)) for i in pipe])

    xga, xgb, lat = call(
        latent_kernel,
        [((TOKENS, WIDTH), BF16), ((TOKENS, WIDTH), BF16), ((PADDED, 2 * UNITS + 128), F32)],
        flops=2 * 2 * TOKENS * WIDTH * UNITS,
        name="latent",
    )(xa, xb, gain, wc)
    keep, send = call(
        code_kernel,
        [((HALF, SUM_COLS), F32), ((HALF, SUM_COLS), BF16)],
        [((PADDED, 2 * UNITS), F32)],
        flops=2 * 2 * TOKENS * WIDTH * UNITS,
        name="code",
    )(ca, cb, we, lat)
    own, *parts = call(
        scatter_kernel,
        [((PART, SUM_COLS), F32)] + [((PART, SUM_COLS), BF16)] * 3,
        [((HALF, SUM_COLS), F32)],
        name="scatter",
    )(keep, swap(send, 1))
    parts = [swap(part, 2 * d) for d, part in zip((1, 2, 3), parts)]
    out, mir = call(
        latent_step_kernel,
        [((PART, OWN_COLS), BF16), ((PART, MIR_COLS), BF16)],
        name="step",
    )(own, *parts, latent_gain)
    mir = lax.ppermute(mir, "pipe", [(i, last - i) for i in pipe])
    out = jnp.concatenate([out, mir], 1)
    (mine,) = call(gather_kernel, [((HALF, ALL_COLS), BF16)], name="gather")(
        out, *(swap(out, 2 * d) for d in (1, 2, 3))
    )
    other = swap(mine, 1)
    big = ((1, TOKENS, WIDTH), BF16)
    grad = ((1, UNITS, WIDTH), BF16)
    return tuple(
        call(
            finish_kernel,
            [big, big, grad, grad],
            [((PADDED, ALL_COLS), BF16)],
            flops=6 * 2 * TOKENS * WIDTH * UNITS,
            name="finish",
        )(mine, other, ca, cb, xa, xb, xga, xm, cm, gain, wc)
    )


def solution(mesh):
    wide = P("pipe", None, "tensor")
    weights = P("pipe", None, None, "tensor")
    return jax.shard_map(
        shards,
        mesh=mesh,
        in_specs=(wide,) * 5 + (P("pipe", None, None), weights, weights),
        out_specs=(wide,) * 4,
        check_vma=False,
    )
```

```python
import jax
import jax.numpy as jnp
from jax import lax
from jax.experimental import pallas as pl
from jax.experimental.pallas import tpu as pltpu
from jax.sharding import PartitionSpec as P

EPSILON = 1e-06
TOKENS = 224
PADDED = 256
HALF = 128
PART = 32
WIDTH = 896
UNITS = 256
FEATURES = 7168
SUM_COLS = 4 * UNITS + 128
OWN_COLS = 3 * UNITS + 128
MIR_COLS = 2 * UNITS
ALL_COLS = OWN_COLS + MIR_COLS
F32 = jnp.float32
BF16 = jnp.bfloat16


def contract_last(left, right):
    return lax.dot_general(left, right, (((1,), (1,)), ((), ())), preferred_element_type=F32)


def contract_first(left, right):
    return lax.dot_general(left, right, (((0,), (0,)), ((), ())), preferred_element_type=F32)


def lanes(rows):
    return lax.broadcasted_iota(jnp.int32, (rows, 128), 1)


def split_pair(first, second):
    lane = lanes(first.shape[0])
    value = jnp.where(lane % 2 == 0, first, second)
    high = value.astype(BF16).astype(F32)
    packed = jnp.where(lane < 2, high, value - high)
    return jnp.where(lane < 4, packed, 0.0).astype(BF16)


def joined(block):
    block = block.astype(F32)
    return block[:, 0:1] + block[:, 2:3], block[:, 1:2] + block[:, 3:4]


def latent_kernel(xa_ref, xb_ref, gain_ref, wc_ref, xga_ref, xgb_ref, lat_ref):
    squares = []
    for s, (x_ref, xg_ref) in enumerate(((xa_ref, xga_ref), (xb_ref, xgb_ref))):
        x = x_ref[0].astype(F32)
        xg = (x * gain_ref[0, s : s + 1, :]).astype(BF16)
        xg_ref[...] = xg
        lat_ref[0:TOKENS, s * UNITS : (s + 1) * UNITS] = contract_last(xg, wc_ref[0, s])
        squares.append(jnp.sum(x * x, -1, keepdims=True))
    lane = lanes(TOKENS)
    block = jnp.where(lane == 0, squares[0], jnp.where(lane == 1, squares[1], 0.0))
    lat_ref[0:TOKENS, 2 * UNITS :] = block
    lat_ref[TOKENS:, :] = jnp.zeros((PADDED - TOKENS, 2 * UNITS + 128), F32)


def code_kernel(ca_ref, cb_ref, we_ref, lat_ref, keep_ref, send_ref, full):
    for s, c_ref in enumerate((ca_ref, cb_ref)):
        full[0:TOKENS, s * UNITS : (s + 1) * UNITS] = contract_last(c_ref[0], we_ref[0, s])
    full[TOKENS:, :] = jnp.zeros((PADDED - TOKENS, 2 * UNITS), F32)
    core = lax.rem(lax.axis_index("tensor"), 2)
    mine = pl.ds(pl.multiple_of(core * HALF, HALF), HALF)
    other = pl.ds(pl.multiple_of((1 - core) * HALF, HALF), HALF)
    keep_ref[:, 0 : 2 * UNITS] = lat_ref[mine, 0 : 2 * UNITS]
    keep_ref[:, 2 * UNITS : 4 * UNITS] = full[mine, :]
    keep_ref[:, 4 * UNITS :] = lat_ref[mine, 2 * UNITS :]
    send_ref[:, 0 : 2 * UNITS] = lat_ref[other, 0 : 2 * UNITS].astype(BF16)
    send_ref[:, 2 * UNITS : 4 * UNITS] = full[other, :].astype(BF16)
    block = lat_ref[other, 2 * UNITS :]
    send_ref[:, 4 * UNITS :] = split_pair(block[:, 0:1], block[:, 1:2])


def scatter_kernel(keep_ref, recv_ref, own_ref, one_ref, two_ref, three_ref, total):
    total[...] = keep_ref[...] + recv_ref[...].astype(F32)
    spot = lax.div(lax.axis_index("tensor"), 2)

    def rows(d):
        return pl.ds(pl.multiple_of((spot ^ d) * PART, PART), PART)

    own_ref[...] = total[rows(0), :]
    for d, ref in ((1, one_ref), (2, two_ref), (3, three_ref)):
        ref[:, 0 : 4 * UNITS] = total[rows(d), 0 : 4 * UNITS].astype(BF16)
        ref[:, 4 * UNITS :] = split_pair(*joined(total[rows(d), 4 * UNITS :]))


def latent_backward(latent_sum, grad_code, square, latent_gain):
    rms = jnp.sqrt(square / FEATURES + EPSILON)
    latent = latent_sum / rms
    latent_rms = jnp.sqrt(jnp.mean(latent * latent, -1, keepdims=True) + EPSILON)
    latent_unit = latent / latent_rms
    code = (latent_unit * latent_gain).astype(BF16)
    grad_unit = grad_code * latent_gain
    latent_centre = jnp.mean(grad_unit * latent_unit, -1, keepdims=True)
    grad_latent = (grad_unit - latent_unit * latent_centre) / latent_rms
    ratio = (grad_latent / rms).astype(BF16)
    centre = jnp.sum(ratio.astype(F32) * latent, -1, keepdims=True) / FEATURES / rms
    return ratio, code, centre


def latent_step_kernel(own_ref, one_ref, two_ref, three_ref, gain_ref, out_ref, mir_ref):
    total = own_ref[...]
    for ref in (one_ref, two_ref, three_ref):
        total = total + ref[...].astype(F32)
    square_a, square_b = joined(total[:, 4 * UNITS :])
    ratio_a, code_a, centre_a = latent_backward(
        total[:, 0:UNITS], total[:, 2 * UNITS : 3 * UNITS], square_a, gain_ref[0, 0:1, :]
    )
    ratio_b, code_b, centre_b = latent_backward(
        total[:, UNITS : 2 * UNITS], total[:, 3 * UNITS : 4 * UNITS], square_b, gain_ref[0, 1:2, :]
    )
    out_ref[:, 0:UNITS] = ratio_a
    out_ref[:, UNITS : 2 * UNITS] = code_a
    out_ref[:, 2 * UNITS : 3 * UNITS] = ratio_b
    out_ref[:, 3 * UNITS :] = split_pair(centre_a, centre_b)
    mir_ref[:, 0:UNITS] = ratio_b
    mir_ref[:, UNITS:] = code_b


def gather_kernel(own_ref, one_ref, two_ref, three_ref, out_ref):
    spot = lax.div(lax.axis_index("tensor"), 2)
    for d, ref in enumerate((own_ref, one_ref, two_ref, three_ref)):
        out_ref[pl.ds(pl.multiple_of((spot ^ d) * PART, PART), PART), :] = ref[...]


def finish_kernel(
    mine_ref, other_ref, ca_ref, cb_ref, xa_ref, xb_ref, xga_ref, xm_ref, cm_ref, gain_ref, wc_ref,
    ia_ref, ib_ref, gc_ref, ge_ref, full,
):
    core = lax.rem(lax.axis_index("tensor"), 2)
    full[pl.ds(pl.multiple_of(core * HALF, HALF), HALF), :] = mine_ref[...]
    full[pl.ds(pl.multiple_of((1 - core) * HALF, HALF), HALF), :] = other_ref[...]
    ratio_a = full[0:TOKENS, 0:UNITS]
    code_a = full[0:TOKENS, UNITS : 2 * UNITS]
    ratio_b = full[0:TOKENS, 2 * UNITS : 3 * UNITS]
    centres = joined(full[0:TOKENS, 3 * UNITS : OWN_COLS])
    ratio_m = full[0:TOKENS, OWN_COLS : OWN_COLS + UNITS]
    code_m = full[0:TOKENS, OWN_COLS + UNITS :]
    streams = ((ratio_a, ca_ref, xa_ref, ia_ref), (ratio_b, cb_ref, xb_ref, ib_ref))
    for s, (ratio, c_ref, x_ref, i_ref) in enumerate(streams):
        grad = jnp.dot(ratio, wc_ref[0, s], preferred_element_type=F32) * gain_ref[0, s : s + 1, :]
        i_ref[0] = (
            c_ref[0].astype(F32) + (grad - x_ref[0].astype(F32) * centres[s])
        ).astype(BF16)
    xg_m = (xm_ref[0].astype(F32) * gain_ref[0, 0:1, :]).astype(BF16)
    mirror = contract_first(ratio_m, xg_m).astype(BF16).astype(F32)
    gc_ref[0] = (contract_first(ratio_a, xga_ref[...]) + mirror).astype(BF16)
    mirror = contract_first(code_m, cm_ref[0]).astype(BF16).astype(F32)
    ge_ref[0] = (contract_first(code_a, ca_ref[0]) + mirror).astype(BF16)


def call(kernel, outs, scratch=(), flops=0, name=None):
    return pl.pallas_call(
        kernel,
        out_shape=[jax.ShapeDtypeStruct(shape, dtype) for shape, dtype in outs],
        scratch_shapes=[pltpu.VMEM(shape, dtype) for shape, dtype in scratch],
        compiler_params=pltpu.CompilerParams(vmem_limit_bytes=40 * 2**20),
        cost_estimate=pl.CostEstimate(flops=flops, bytes_accessed=4 * 2**20, transcendentals=0),
        name=name,
    )


def shards(xa, xb, sent_a, sent_b, gain, latent_gain, wc, we):
    pipe = range(lax.axis_size("pipe"))
    last = len(pipe) - 1
    tensor = range(lax.axis_size("tensor"))

    def swap(value, d):
        return lax.ppermute(value, "tensor", [(i, i ^ d) for i in tensor])

    ca = lax.ppermute(sent_a, "pipe", [((i + 1) % len(pipe), i) for i in pipe])
    cb = lax.ppermute(sent_b, "pipe", [(i, (i + 1) % len(pipe)) for i in pipe])
    half = len(pipe) // 2
    xm = lax.ppermute(xb, "pipe", [(i, i ^ half) for i in pipe])
    cm = lax.ppermute(
        sent_b, "pipe", [(i, i if i % half == half - 1 else i - i % half + half - 2 - i % half) for i in pipe]
    )

    xga, xgb, lat = call(
        latent_kernel,
        [((TOKENS, WIDTH), BF16), ((TOKENS, WIDTH), BF16), ((PADDED, 2 * UNITS + 128), F32)],
        flops=2 * 2 * TOKENS * WIDTH * UNITS,
        name="latent",
    )(xa, xb, gain, wc)
    keep, send = call(
        code_kernel,
        [((HALF, SUM_COLS), F32), ((HALF, SUM_COLS), BF16)],
        [((PADDED, 2 * UNITS), F32)],
        flops=2 * 2 * TOKENS * WIDTH * UNITS,
        name="code",
    )(ca, cb, we, lat)
    own, *parts = call(
        scatter_kernel,
        [((PART, SUM_COLS), F32)] + [((PART, SUM_COLS), BF16)] * 3,
        [((HALF, SUM_COLS), F32)],
        name="scatter",
    )(keep, swap(send, 1))
    parts = [swap(part, 2 * d) for d, part in zip((1, 2, 3), parts)]
    out, mir = call(
        latent_step_kernel,
        [((PART, OWN_COLS), BF16), ((PART, MIR_COLS), BF16)],
        name="step",
    )(own, *parts, latent_gain)
    xm, cm, mir = lax.optimization_barrier((xm, cm, mir))
    xm = lax.ppermute(xm, "pipe", [(i, i ^ (half - 1)) for i in pipe])
    cm = lax.ppermute(cm, "pipe", [(i, i if i % half == half - 1 else i ^ half) for i in pipe])
    mir = lax.ppermute(mir, "pipe", [(i, last - i) for i in pipe])
    out = jnp.concatenate([out, mir], 1)
    (mine,) = call(gather_kernel, [((HALF, ALL_COLS), BF16)], name="gather")(
        out, *(swap(out, 2 * d) for d in (1, 2, 3))
    )
    mine, xm, cm = lax.optimization_barrier((mine, xm, cm))
    other = swap(mine, 1)
    big = ((1, TOKENS, WIDTH), BF16)
    grad = ((1, UNITS, WIDTH), BF16)
    return tuple(
        call(
            finish_kernel,
            [big, big, grad, grad],
            [((PADDED, ALL_COLS), BF16)],
            flops=6 * 2 * TOKENS * WIDTH * UNITS,
            name="finish",
        )(mine, other, ca, cb, xa, xb, xga, xm, cm, gain, wc)
    )


def solution(mesh):
    wide = P("pipe", None, "tensor")
    weights = P("pipe", None, None, "tensor")
    return jax.shard_map(
        shards,
        mesh=mesh,
        in_specs=(wide,) * 5 + (P("pipe", None, None), weights, weights),
        out_specs=(wide,) * 4,
        check_vma=False,
    )
```

```python
import jax
import jax.numpy as jnp
from jax import lax
from jax.experimental import pallas as pl
from jax.experimental.pallas import tpu as pltpu
from jax.sharding import PartitionSpec as P

EPSILON = 1e-06
TOKENS = 224
PADDED = 256
HALF = 128
PART = 32
WIDTH = 896
UNITS = 256
FEATURES = 7168
SUM_COLS = 4 * UNITS + 128
OWN_COLS = 3 * UNITS + 128
MIR_COLS = 2 * UNITS
ALL_COLS = OWN_COLS + MIR_COLS
F32 = jnp.float32
BF16 = jnp.bfloat16


def contract_last(left, right):
    return lax.dot_general(left, right, (((1,), (1,)), ((), ())), preferred_element_type=F32)


def contract_first(left, right):
    return lax.dot_general(left, right, (((0,), (0,)), ((), ())), preferred_element_type=F32)


def lanes(rows):
    return lax.broadcasted_iota(jnp.int32, (rows, 128), 1)


def split_pair(first, second):
    lane = lanes(first.shape[0])
    value = jnp.where(lane % 2 == 0, first, second)
    high = value.astype(BF16).astype(F32)
    packed = jnp.where(lane < 2, high, value - high)
    return jnp.where(lane < 4, packed, 0.0).astype(BF16)


def joined(block):
    block = block.astype(F32)
    return block[:, 0:1] + block[:, 2:3], block[:, 1:2] + block[:, 3:4]


def latent_kernel(xa_ref, xb_ref, gain_ref, wc_ref, xga_ref, lat_ref):
    squares = []
    for s, x_ref in enumerate((xa_ref, xb_ref)):
        x = x_ref[0].astype(F32)
        xg = (x * gain_ref[0, s : s + 1, :]).astype(BF16)
        if s == 0:
            xga_ref[...] = xg
        lat_ref[0:TOKENS, s * UNITS : (s + 1) * UNITS] = contract_last(xg, wc_ref[0, s])
        squares.append(jnp.sum(x * x, -1, keepdims=True))
    lane = lanes(TOKENS)
    block = jnp.where(lane == 0, squares[0], jnp.where(lane == 1, squares[1], 0.0))
    lat_ref[0:TOKENS, 2 * UNITS :] = block
    lat_ref[TOKENS:, :] = jnp.zeros((PADDED - TOKENS, 2 * UNITS + 128), F32)


def place_and_end():
    half = lax.axis_size("pipe") // 2
    return lax.rem(lax.axis_index("pipe"), half), half - 1


def code_kernel(ca_ref, cb_ref, sa_ref, sb_ref, we_ref, lat_ref, keep_ref, send_ref, full):
    place, end = place_and_end()
    full[0:TOKENS, 0:UNITS] = contract_last(
        jnp.where(place == end, sb_ref[0], ca_ref[0]), we_ref[0, 0]
    )
    full[0:TOKENS, UNITS:] = contract_last(
        jnp.where(place == 0, sa_ref[0], cb_ref[0]), we_ref[0, 1]
    )
    full[TOKENS:, :] = jnp.zeros((PADDED - TOKENS, 2 * UNITS), F32)
    core = lax.rem(lax.axis_index("tensor"), 2)
    mine = pl.ds(pl.multiple_of(core * HALF, HALF), HALF)
    other = pl.ds(pl.multiple_of((1 - core) * HALF, HALF), HALF)
    keep_ref[:, 0 : 2 * UNITS] = lat_ref[mine, 0 : 2 * UNITS]
    keep_ref[:, 2 * UNITS : 4 * UNITS] = full[mine, :]
    keep_ref[:, 4 * UNITS :] = lat_ref[mine, 2 * UNITS :]
    send_ref[:, 0 : 2 * UNITS] = lat_ref[other, 0 : 2 * UNITS].astype(BF16)
    send_ref[:, 2 * UNITS : 4 * UNITS] = full[other, :].astype(BF16)
    block = lat_ref[other, 2 * UNITS :]
    send_ref[:, 4 * UNITS :] = split_pair(block[:, 0:1], block[:, 1:2])


def scatter_kernel(keep_ref, recv_ref, own_ref, one_ref, two_ref, three_ref, total):
    total[...] = keep_ref[...] + recv_ref[...].astype(F32)
    spot = lax.div(lax.axis_index("tensor"), 2)

    def rows(d):
        return pl.ds(pl.multiple_of((spot ^ d) * PART, PART), PART)

    own_ref[...] = total[rows(0), :]
    for d, ref in ((1, one_ref), (2, two_ref), (3, three_ref)):
        ref[:, 0 : 4 * UNITS] = total[rows(d), 0 : 4 * UNITS].astype(BF16)
        ref[:, 4 * UNITS :] = split_pair(*joined(total[rows(d), 4 * UNITS :]))


def latent_backward(latent_sum, grad_code, square, latent_gain):
    rms = jnp.sqrt(square / FEATURES + EPSILON)
    latent = latent_sum / rms
    latent_rms = jnp.sqrt(jnp.mean(latent * latent, -1, keepdims=True) + EPSILON)
    latent_unit = latent / latent_rms
    code = (latent_unit * latent_gain).astype(BF16)
    grad_unit = grad_code * latent_gain
    latent_centre = jnp.mean(grad_unit * latent_unit, -1, keepdims=True)
    grad_latent = (grad_unit - latent_unit * latent_centre) / latent_rms
    ratio = (grad_latent / rms).astype(BF16)
    centre = jnp.sum(ratio.astype(F32) * latent, -1, keepdims=True) / FEATURES / rms
    return ratio, code, centre


def sum_kernel(own_ref, one_ref, two_ref, three_ref, total_ref, swap_ref):
    total = own_ref[...]
    for ref in (one_ref, two_ref, three_ref):
        total = total + ref[...].astype(F32)
    total_ref[...] = total
    swap_ref[:, 0:UNITS] = total[:, UNITS : 2 * UNITS].astype(BF16)
    swap_ref[:, UNITS : 2 * UNITS] = total[:, 3 * UNITS : 4 * UNITS].astype(BF16)
    swap_ref[:, 2 * UNITS : 3 * UNITS] = total[:, 2 * UNITS : 3 * UNITS].astype(BF16)
    swap_ref[:, 3 * UNITS :] = split_pair(*joined(total[:, 4 * UNITS :]))


def latent_step_kernel(total_ref, far_ref, gain_ref, out_ref):
    place, end = place_and_end()
    square_a, square_b = joined(total_ref[:, 4 * UNITS :])
    _, square_m = joined(far_ref[:, 3 * UNITS :])
    own_a = total_ref[:, 2 * UNITS : 3 * UNITS]
    own_b = total_ref[:, 3 * UNITS : 4 * UNITS]
    far_b = far_ref[:, UNITS : 2 * UNITS].astype(F32)
    far_a = far_ref[:, 2 * UNITS : 3 * UNITS].astype(F32)
    gain_a, gain_b = gain_ref[0, 0:1, :], gain_ref[0, 1:2, :]
    ratio_a, code_a, centre_a = latent_backward(
        total_ref[:, 0:UNITS], jnp.where(place == end, far_b, own_a), square_a, gain_a
    )
    ratio_b, _, centre_b = latent_backward(
        total_ref[:, UNITS : 2 * UNITS], jnp.where(place == 0, far_a, own_b), square_b, gain_b
    )
    ratio_m, code_m, _ = latent_backward(
        far_ref[:, 0:UNITS].astype(F32), jnp.where(place == end, own_a, far_b), square_m, gain_a
    )
    out_ref[:, 0:UNITS] = ratio_a
    out_ref[:, UNITS : 2 * UNITS] = code_a
    out_ref[:, 2 * UNITS : 3 * UNITS] = ratio_b
    out_ref[:, 3 * UNITS : OWN_COLS] = split_pair(centre_a, centre_b)
    out_ref[:, OWN_COLS : OWN_COLS + UNITS] = ratio_m
    out_ref[:, OWN_COLS + UNITS :] = code_m


def gather_kernel(own_ref, one_ref, two_ref, three_ref, out_ref):
    spot = lax.div(lax.axis_index("tensor"), 2)
    for d, ref in enumerate((own_ref, one_ref, two_ref, three_ref)):
        out_ref[pl.ds(pl.multiple_of((spot ^ d) * PART, PART), PART), :] = ref[...]


def finish_kernel(
    mine_ref, other_ref, ca_ref, cb_ref, far_a_ref, far_b_ref, xa_ref, xb_ref, xga_ref, xm_ref,
    cm_ref, gain_ref, wc_ref,
    ia_ref, ib_ref, gc_ref, ge_ref, full,
):
    core = lax.rem(lax.axis_index("tensor"), 2)
    full[pl.ds(pl.multiple_of(core * HALF, HALF), HALF), :] = mine_ref[...]
    full[pl.ds(pl.multiple_of((1 - core) * HALF, HALF), HALF), :] = other_ref[...]
    ratio_a = full[0:TOKENS, 0:UNITS]
    code_a = full[0:TOKENS, UNITS : 2 * UNITS]
    ratio_b = full[0:TOKENS, 2 * UNITS : 3 * UNITS]
    centres = joined(full[0:TOKENS, 3 * UNITS : OWN_COLS])
    ratio_m = full[0:TOKENS, OWN_COLS : OWN_COLS + UNITS]
    code_m = full[0:TOKENS, OWN_COLS + UNITS :]
    place, end = place_and_end()
    cot_a = jnp.where(place == end, far_a_ref[0], ca_ref[0])
    cot_b = jnp.where(place == 0, far_b_ref[0], cb_ref[0])
    streams = ((ratio_a, cot_a, xa_ref, ia_ref), (ratio_b, cot_b, xb_ref, ib_ref))
    for s, (ratio, cot, x_ref, i_ref) in enumerate(streams):
        grad = jnp.dot(ratio, wc_ref[0, s], preferred_element_type=F32) * gain_ref[0, s : s + 1, :]
        i_ref[0] = (
            cot.astype(F32) + (grad - x_ref[0].astype(F32) * centres[s])
        ).astype(BF16)
    xg_m = (xm_ref[0].astype(F32) * gain_ref[0, 0:1, :]).astype(BF16)
    mirror = contract_first(ratio_m, xg_m).astype(BF16).astype(F32)
    gc_ref[0] = (contract_first(ratio_a, xga_ref[...]) + mirror).astype(BF16)
    mirror = contract_first(code_m, cm_ref[0]).astype(BF16).astype(F32)
    ge_ref[0] = (contract_first(code_a, cot_a) + mirror).astype(BF16)


def call(kernel, outs, scratch=(), flops=0, name=None):
    return pl.pallas_call(
        kernel,
        out_shape=[jax.ShapeDtypeStruct(shape, dtype) for shape, dtype in outs],
        scratch_shapes=[pltpu.VMEM(shape, dtype) for shape, dtype in scratch],
        compiler_params=pltpu.CompilerParams(vmem_limit_bytes=40 * 2**20),
        cost_estimate=pl.CostEstimate(flops=flops, bytes_accessed=4 * 2**20, transcendentals=0),
        name=name,
    )


def shards(xa, xb, sent_a, sent_b, gain, latent_gain, wc, we):
    pipe = range(lax.axis_size("pipe"))
    last = len(pipe) - 1
    tensor = range(lax.axis_size("tensor"))

    def swap(value, d):
        return lax.ppermute(value, "tensor", [(i, i ^ d) for i in tensor])

    half = len(pipe) // 2

    def flip_x(value):
        return lax.ppermute(value, "pipe", [(i, i ^ half) for i in pipe])

    def turn_x(value):
        return lax.ppermute(value, "pipe", [(i, i ^ (half - 1)) for i in pipe])

    def flip_c(value):
        return lax.ppermute(value, "pipe", [(i, i if i % half == half - 1 else i ^ half) for i in pipe])

    def turn_c(value):
        pairs = [(i, i - i % half + (half - 2 - i % half) % half) for i in pipe]
        return lax.ppermute(value, "pipe", pairs)

    cb = lax.ppermute(sent_b, "pipe", [(i - 1, i) for i in pipe if i % half != 0])
    def end_flip(value):
        return lax.ppermute(value, "pipe", [(i, i ^ half) for i in pipe if i % half == half - 1])

    ca = lax.ppermute(sent_a, "pipe", [(i + 1, i) for i in pipe if i % half != half - 1])
    xm = flip_x(xb)

    far_a = lax.ppermute(sent_a, "pipe", [(i, i + half - 1) for i in pipe if i % half == 0])
    xga, lat = call(
        latent_kernel,
        [((TOKENS, WIDTH), BF16), ((PADDED, 2 * UNITS + 128), F32)],
        flops=2 * 2 * TOKENS * WIDTH * UNITS,
        name="latent",
    )(xa, xb, gain, wc)
    lat, ca, far = lax.optimization_barrier((lat, ca, sent_b))
    cm = turn_c(far)
    keep, send = call(
        code_kernel,
        [((HALF, SUM_COLS), F32), ((HALF, SUM_COLS), BF16)],
        [((PADDED, 2 * UNITS), F32)],
        flops=2 * 2 * TOKENS * WIDTH * UNITS,
        name="code",
    )(ca, cb, sent_a, sent_b, we, lat)
    recv = swap(send, 1)
    recv, far_a = lax.optimization_barrier((recv, far_a))
    own, *parts = call(
        scatter_kernel,
        [((PART, SUM_COLS), F32)] + [((PART, SUM_COLS), BF16)] * 3,
        [((HALF, SUM_COLS), F32)],
        name="scatter",
    )(keep, recv)
    parts = [swap(part, 2 * d) for d, part in zip((1, 2, 3), parts)]
    total, mir = call(
        sum_kernel,
        [((PART, SUM_COLS), F32), ((PART, OWN_COLS), BF16)],
        name="sum",
    )(own, *parts)
    mir, xm, cm, end_b = lax.optimization_barrier((mir, xm, cm, sent_b))
    far_b = end_flip(end_b)
    xm = turn_x(xm)
    cm = flip_c(cm)
    mir = lax.ppermute(mir, "pipe", [(i, last - i) for i in pipe])
    (out,) = call(latent_step_kernel, [((PART, ALL_COLS), BF16)], name="step")(
        total, mir, latent_gain
    )
    out, xm, cm = lax.optimization_barrier((out, xm, cm))
    far_b = lax.ppermute(far_b, "pipe", [(i, i - half + 1) for i in pipe if i % half == half - 1])
    far_a = end_flip(far_a)
    (mine,) = call(gather_kernel, [((HALF, ALL_COLS), BF16)], name="gather")(
        out, *(swap(out, 2 * d) for d in (1, 2, 3))
    )
    other = swap(mine, 1)
    big = ((1, TOKENS, WIDTH), BF16)
    grad = ((1, UNITS, WIDTH), BF16)
    return tuple(
        call(
            finish_kernel,
            [big, big, grad, grad],
            [((PADDED, ALL_COLS), BF16)],
            flops=6 * 2 * TOKENS * WIDTH * UNITS,
            name="finish",
        )(mine, other, ca, cb, far_a, far_b, xa, xb, xga, xm, cm, gain, wc)
    )


def solution(mesh):
    wide = P("pipe", None, "tensor")
    weights = P("pipe", None, None, "tensor")
    return jax.shard_map(
        shards,
        mesh=mesh,
        in_specs=(wide,) * 5 + (P("pipe", None, None), weights, weights),
        out_specs=(wide,) * 4,
        check_vma=False,
    )
```

```python
import jax
import jax.numpy as jnp
from jax import lax
from jax.experimental import pallas as pl
from jax.experimental.pallas import tpu as pltpu
from jax.sharding import PartitionSpec as P

EPSILON = 1e-06
TOKENS = 224
PADDED = 256
HALF = 128
PART = 32
WIDTH = 896
UNITS = 256
FEATURES = 7168
SUM_COLS = 4 * UNITS + 128
OWN_COLS = 3 * UNITS + 128
MIR_COLS = 2 * UNITS
ALL_COLS = OWN_COLS + MIR_COLS
F32 = jnp.float32
BF16 = jnp.bfloat16


def contract_last(left, right):
    return lax.dot_general(left, right, (((1,), (1,)), ((), ())), preferred_element_type=F32)


def contract_first(left, right):
    return lax.dot_general(left, right, (((0,), (0,)), ((), ())), preferred_element_type=F32)


def lanes(rows):
    return lax.broadcasted_iota(jnp.int32, (rows, 128), 1)


def split_pair(first, second):
    lane = lanes(first.shape[0])
    value = jnp.where(lane % 2 == 0, first, second)
    high = value.astype(BF16).astype(F32)
    packed = jnp.where(lane < 2, high, value - high)
    return jnp.where(lane < 4, packed, 0.0).astype(BF16)


def joined(block):
    block = block.astype(F32)
    return block[:, 0:1] + block[:, 2:3], block[:, 1:2] + block[:, 3:4]


def latent_kernel(xa_ref, xb_ref, gain_ref, wc_ref, xga_ref, lat_ref):
    squares = []
    for s, x_ref in enumerate((xa_ref, xb_ref)):
        x = x_ref[0].astype(F32)
        scaled = x * gain_ref[0, s : s + 1, :]
        xg = scaled.astype(BF16)
        rest = (scaled - xg.astype(F32)).astype(BF16)
        if s == 0:
            xga_ref[...] = xg
        lat_ref[0:TOKENS, s * UNITS : (s + 1) * UNITS] = contract_last(
            xg, wc_ref[0, s]
        ) + contract_last(rest, wc_ref[0, s])
        squares.append(jnp.sum(x * x, -1, keepdims=True))
    lane = lanes(TOKENS)
    block = jnp.where(lane == 0, squares[0], jnp.where(lane == 1, squares[1], 0.0))
    lat_ref[0:TOKENS, 2 * UNITS :] = block
    lat_ref[TOKENS:, :] = jnp.zeros((PADDED - TOKENS, 2 * UNITS + 128), F32)


def place_and_end():
    half = lax.axis_size("pipe") // 2
    return lax.rem(lax.axis_index("pipe"), half), half - 1


def code_kernel(ca_ref, cb_ref, sa_ref, sb_ref, we_ref, lat_ref, keep_ref, send_ref, full):
    place, end = place_and_end()
    full[0:TOKENS, 0:UNITS] = contract_last(
        jnp.where(place == end, sb_ref[0], ca_ref[0]), we_ref[0, 0]
    )
    full[0:TOKENS, UNITS:] = contract_last(
        jnp.where(place == 0, sa_ref[0], cb_ref[0]), we_ref[0, 1]
    )
    full[TOKENS:, :] = jnp.zeros((PADDED - TOKENS, 2 * UNITS), F32)
    core = lax.rem(lax.axis_index("tensor"), 2)
    mine = pl.ds(pl.multiple_of(core * HALF, HALF), HALF)
    other = pl.ds(pl.multiple_of((1 - core) * HALF, HALF), HALF)
    keep_ref[:, 0 : 2 * UNITS] = lat_ref[mine, 0 : 2 * UNITS]
    keep_ref[:, 2 * UNITS : 4 * UNITS] = full[mine, :]
    keep_ref[:, 4 * UNITS :] = lat_ref[mine, 2 * UNITS :]
    send_ref[:, 0 : 2 * UNITS] = lat_ref[other, 0 : 2 * UNITS].astype(BF16)
    send_ref[:, 2 * UNITS : 4 * UNITS] = full[other, :].astype(BF16)
    block = lat_ref[other, 2 * UNITS :]
    send_ref[:, 4 * UNITS :] = split_pair(block[:, 0:1], block[:, 1:2])


def scatter_kernel(keep_ref, recv_ref, own_ref, one_ref, two_ref, three_ref, total):
    total[...] = keep_ref[...] + recv_ref[...].astype(F32)
    spot = lax.div(lax.axis_index("tensor"), 2)

    def rows(d):
        return pl.ds(pl.multiple_of((spot ^ d) * PART, PART), PART)

    own_ref[...] = total[rows(0), :]
    for d, ref in ((1, one_ref), (2, two_ref), (3, three_ref)):
        ref[:, 0 : 4 * UNITS] = total[rows(d), 0 : 4 * UNITS].astype(BF16)
        ref[:, 4 * UNITS :] = split_pair(*joined(total[rows(d), 4 * UNITS :]))


def latent_backward(latent_sum, grad_code, square, latent_gain):
    rms = jnp.sqrt(square / FEATURES + EPSILON)
    latent = latent_sum / rms
    latent_rms = jnp.sqrt(jnp.mean(latent * latent, -1, keepdims=True) + EPSILON)
    latent_unit = latent / latent_rms
    code = (latent_unit * latent_gain).astype(BF16)
    grad_unit = grad_code * latent_gain
    latent_centre = jnp.mean(grad_unit * latent_unit, -1, keepdims=True)
    grad_latent = (grad_unit - latent_unit * latent_centre) / latent_rms
    ratio = (grad_latent / rms).astype(BF16)
    centre = jnp.sum(ratio.astype(F32) * latent, -1, keepdims=True) / FEATURES / rms
    return ratio, code, centre


def sum_kernel(own_ref, one_ref, two_ref, three_ref, total_ref, swap_ref):
    total = own_ref[...]
    for ref in (one_ref, two_ref, three_ref):
        total = total + ref[...].astype(F32)
    total_ref[...] = total
    swap_ref[:, 0:UNITS] = total[:, UNITS : 2 * UNITS].astype(BF16)
    swap_ref[:, UNITS : 2 * UNITS] = total[:, 3 * UNITS : 4 * UNITS].astype(BF16)
    swap_ref[:, 2 * UNITS : 3 * UNITS] = total[:, 2 * UNITS : 3 * UNITS].astype(BF16)
    swap_ref[:, 3 * UNITS :] = split_pair(*joined(total[:, 4 * UNITS :]))


def latent_step_kernel(total_ref, far_ref, gain_ref, out_ref):
    place, end = place_and_end()
    square_a, square_b = joined(total_ref[:, 4 * UNITS :])
    _, square_m = joined(far_ref[:, 3 * UNITS :])
    own_a = total_ref[:, 2 * UNITS : 3 * UNITS]
    own_b = total_ref[:, 3 * UNITS : 4 * UNITS]
    far_b = far_ref[:, UNITS : 2 * UNITS].astype(F32)
    far_a = far_ref[:, 2 * UNITS : 3 * UNITS].astype(F32)
    gain_a, gain_b = gain_ref[0, 0:1, :], gain_ref[0, 1:2, :]
    ratio_a, code_a, centre_a = latent_backward(
        total_ref[:, 0:UNITS], jnp.where(place == end, far_b, own_a), square_a, gain_a
    )
    ratio_b, _, centre_b = latent_backward(
        total_ref[:, UNITS : 2 * UNITS], jnp.where(place == 0, far_a, own_b), square_b, gain_b
    )
    ratio_m, code_m, _ = latent_backward(
        far_ref[:, 0:UNITS].astype(F32), jnp.where(place == end, own_a, far_b), square_m, gain_a
    )
    out_ref[:, 0:UNITS] = ratio_a
    out_ref[:, UNITS : 2 * UNITS] = code_a
    out_ref[:, 2 * UNITS : 3 * UNITS] = ratio_b
    out_ref[:, 3 * UNITS : OWN_COLS] = split_pair(centre_a, centre_b)
    out_ref[:, OWN_COLS : OWN_COLS + UNITS] = ratio_m
    out_ref[:, OWN_COLS + UNITS :] = code_m


def gather_kernel(own_ref, one_ref, two_ref, three_ref, out_ref):
    spot = lax.div(lax.axis_index("tensor"), 2)
    for d, ref in enumerate((own_ref, one_ref, two_ref, three_ref)):
        out_ref[pl.ds(pl.multiple_of((spot ^ d) * PART, PART), PART), :] = ref[...]


def finish_kernel(
    mine_ref, other_ref, ca_ref, cb_ref, far_a_ref, far_b_ref, xa_ref, xb_ref, xga_ref, xm_ref,
    cm_ref, gain_ref, wc_ref,
    ia_ref, ib_ref, gc_ref, ge_ref, full,
):
    core = lax.rem(lax.axis_index("tensor"), 2)
    full[pl.ds(pl.multiple_of(core * HALF, HALF), HALF), :] = mine_ref[...]
    full[pl.ds(pl.multiple_of((1 - core) * HALF, HALF), HALF), :] = other_ref[...]
    ratio_a = full[0:TOKENS, 0:UNITS]
    code_a = full[0:TOKENS, UNITS : 2 * UNITS]
    ratio_b = full[0:TOKENS, 2 * UNITS : 3 * UNITS]
    centres = joined(full[0:TOKENS, 3 * UNITS : OWN_COLS])
    ratio_m = full[0:TOKENS, OWN_COLS : OWN_COLS + UNITS]
    code_m = full[0:TOKENS, OWN_COLS + UNITS :]
    place, end = place_and_end()
    cot_a = jnp.where(place == end, far_a_ref[0], ca_ref[0])
    cot_b = jnp.where(place == 0, far_b_ref[0], cb_ref[0])
    streams = ((ratio_a, cot_a, xa_ref, ia_ref), (ratio_b, cot_b, xb_ref, ib_ref))
    for s, (ratio, cot, x_ref, i_ref) in enumerate(streams):
        grad = jnp.dot(ratio, wc_ref[0, s], preferred_element_type=F32) * gain_ref[0, s : s + 1, :]
        i_ref[0] = (
            cot.astype(F32) + (grad - x_ref[0].astype(F32) * centres[s])
        ).astype(BF16)
    xg_m = (xm_ref[0].astype(F32) * gain_ref[0, 0:1, :]).astype(BF16)
    mirror = contract_first(ratio_m, xg_m).astype(BF16).astype(F32)
    gc_ref[0] = (contract_first(ratio_a, xga_ref[...]) + mirror).astype(BF16)
    mirror = contract_first(code_m, cm_ref[0]).astype(BF16).astype(F32)
    ge_ref[0] = (contract_first(code_a, cot_a) + mirror).astype(BF16)


def call(kernel, outs, scratch=(), flops=0, name=None):
    return pl.pallas_call(
        kernel,
        out_shape=[jax.ShapeDtypeStruct(shape, dtype) for shape, dtype in outs],
        scratch_shapes=[pltpu.VMEM(shape, dtype) for shape, dtype in scratch],
        compiler_params=pltpu.CompilerParams(vmem_limit_bytes=40 * 2**20),
        cost_estimate=pl.CostEstimate(flops=flops, bytes_accessed=4 * 2**20, transcendentals=0),
        name=name,
    )


def shards(xa, xb, sent_a, sent_b, gain, latent_gain, wc, we):
    pipe = range(lax.axis_size("pipe"))
    last = len(pipe) - 1
    tensor = range(lax.axis_size("tensor"))

    def swap(value, d):
        return lax.ppermute(value, "tensor", [(i, i ^ d) for i in tensor])

    half = len(pipe) // 2

    def flip_x(value):
        return lax.ppermute(value, "pipe", [(i, i ^ half) for i in pipe])

    def turn_x(value):
        return lax.ppermute(value, "pipe", [(i, i ^ (half - 1)) for i in pipe])

    def flip_c(value):
        return lax.ppermute(value, "pipe", [(i, i if i % half == half - 1 else i ^ half) for i in pipe])

    def turn_c(value):
        pairs = [(i, i - i % half + (half - 2 - i % half) % half) for i in pipe]
        return lax.ppermute(value, "pipe", pairs)

    cb = lax.ppermute(sent_b, "pipe", [(i - 1, i) for i in pipe if i % half != 0])
    def end_flip(value):
        return lax.ppermute(value, "pipe", [(i, i ^ half) for i in pipe if i % half == half - 1])

    ca = lax.ppermute(sent_a, "pipe", [(i + 1, i) for i in pipe if i % half != half - 1])
    xm = flip_x(xb)

    far_a = lax.ppermute(sent_a, "pipe", [(i, i + half - 1) for i in pipe if i % half == 0])
    xga, lat = call(
        latent_kernel,
        [((TOKENS, WIDTH), BF16), ((PADDED, 2 * UNITS + 128), F32)],
        flops=2 * 2 * TOKENS * WIDTH * UNITS,
        name="latent",
    )(xa, xb, gain, wc)
    lat, ca, far = lax.optimization_barrier((lat, ca, sent_b))
    cm = turn_c(far)
    keep, send = call(
        code_kernel,
        [((HALF, SUM_COLS), F32), ((HALF, SUM_COLS), BF16)],
        [((PADDED, 2 * UNITS), F32)],
        flops=2 * 2 * TOKENS * WIDTH * UNITS,
        name="code",
    )(ca, cb, sent_a, sent_b, we, lat)
    recv = swap(send, 1)
    recv, far_a = lax.optimization_barrier((recv, far_a))
    own, *parts = call(
        scatter_kernel,
        [((PART, SUM_COLS), F32)] + [((PART, SUM_COLS), BF16)] * 3,
        [((HALF, SUM_COLS), F32)],
        name="scatter",
    )(keep, recv)
    parts = [swap(part, 2 * d) for d, part in zip((1, 2, 3), parts)]
    total, mir = call(
        sum_kernel,
        [((PART, SUM_COLS), F32), ((PART, OWN_COLS), BF16)],
        name="sum",
    )(own, *parts)
    mir, xm, cm, end_b = lax.optimization_barrier((mir, xm, cm, sent_b))
    far_b = end_flip(end_b)
    xm = turn_x(xm)
    cm = flip_c(cm)
    mir = lax.ppermute(mir, "pipe", [(i, last - i) for i in pipe])
    (out,) = call(latent_step_kernel, [((PART, ALL_COLS), BF16)], name="step")(
        total, mir, latent_gain
    )
    out, xm = lax.optimization_barrier((out, xm))
    far_b = lax.ppermute(far_b, "pipe", [(i, i - half + 1) for i in pipe if i % half == half - 1])
    far_a = end_flip(far_a)
    (mine,) = call(gather_kernel, [((HALF, ALL_COLS), BF16)], name="gather")(
        out, *(swap(out, 2 * d) for d in (1, 2, 3))
    )
    mine, cm = lax.optimization_barrier((mine, cm))
    other = swap(mine, 1)
    big = ((1, TOKENS, WIDTH), BF16)
    grad = ((1, UNITS, WIDTH), BF16)
    return tuple(
        call(
            finish_kernel,
            [big, big, grad, grad],
            [((PADDED, ALL_COLS), BF16)],
            flops=6 * 2 * TOKENS * WIDTH * UNITS,
            name="finish",
        )(mine, other, ca, cb, far_a, far_b, xa, xb, xga, xm, cm, gain, wc)
    )


def solution(mesh):
    wide = P("pipe", None, "tensor")
    weights = P("pipe", None, None, "tensor")
    return jax.shard_map(
        shards,
        mesh=mesh,
        in_specs=(wide,) * 5 + (P("pipe", None, None), weights, weights),
        out_specs=(wide,) * 4,
        check_vma=False,
    )
```
